32 devices in a mesh: wide: 16 (over z, y, x), narrow: 2 (over core).
Axes of the slice: x: 2, y: 2, z: 4, core: 2. Of those that a mesh axis runs over, the one named last changes fastest.
Arguments:
- right_side: bfloat16 [4, 1024, 512], P(None, 'wide'), may hold values from -6 to 6
- partial_in: float32 [2, 4, 1024, 512], P('narrow', None, 'wide'), may hold values from -6 to 6
- window_factor: bfloat16 [4, 1024, 4, 1024], P(None, 'wide', None, 'narrow'), may hold values from -0.09375 to 0.09375
- inverse_t: bfloat16 [4, 1024, 1024], P(None, 'wide', 'narrow'), as said below
- trailing_factor: bfloat16 [32768, 4, 1024], P('wide', None, 'narrow'), may hold values from -0.09375 to 0.09375
Outputs:
- solved: bfloat16 [4, 1024, 512], P(None, 'narrow')
- trailing: float32 [32768, 512], P(('wide', 'narrow'))
The draws below stay inside these ranges and needn't reach their ends.
Inputs may be any that keep to these rules, and one draw needn't show every extreme that they name: inverse_t[k] is the transpose of the inverse of the k-th diagonal block of the lower-triangular factor: entry [k, j, i] is zero where j > i.
All inputs are finite; a program needn't handle non-finite values.
Results may differ from the reference program's by a relative error of at most 0.012.
Values may be sent and summed in bfloat16 or wider, within the bound.
A program may use at most 64 MiB of HBM per device.

```python
import math
import jax
import jax.numpy as jnp

NB = 1024
RHS = 512
STEPS = 4
ROWS = 32768
N_NARROW = 2


def draw_inverse_t(key, part):
    key_off, key_diag = jax.random.split(key)
    first = jnp.arange(NB)[:, None]
    second = jnp.arange(NB)[None, :]
    below = (first < second).astype(jnp.float32)
    eye = (first == second).astype(jnp.float32)
    offdiag = jax.random.truncated_normal(key_off, -4.0, 4.0, (STEPS, NB, NB), jnp.float32)
    diag = jax.random.uniform(key_diag, (STEPS, 1, NB), jnp.float32, 0.5, 1.5)
    values = offdiag * below * (0.5 / math.sqrt(NB)) + diag * eye
    return values.astype(jnp.bfloat16)


def shard_levels(rng, shape, cuts, least, largest):
    gain = 1.0
    for position, shards_of in cuts:
        heights = jax.random.uniform(jax.random.fold_in(jax.random.fold_in(rng, 6), position), (shards_of,), jnp.float32, least / len(cuts), largest / len(cuts))
        gain = gain * jnp.repeat(jnp.exp(heights), shape[position] // shards_of).reshape((-1,) + (1,) * (len(shape) - 1 - position))
    return gain


def centred(stream_key, extent, spread, limit, shards=(), dtype=jnp.bfloat16):
    level = shard_levels(stream_key, extent, shards, -0.22, 0.18) if shards else 1.0
    entries = jax.random.normal(stream_key, extent, jnp.float32) * spread * level
    return jnp.minimum(jnp.maximum(entries, -limit), limit).astype(dtype)


def setup_inputs(seed: int = 0) -> dict:
    streams_of = jax.random.split(jax.random.key(seed), 6)
    right_side = centred(streams_of[0], (STEPS, NB, RHS), 1.0, 6.0, ((1, 16),))
    partial_in = centred(streams_of[1], (N_NARROW, STEPS, NB, RHS), 1.0, 6.0, ((0, 2), (2, 16)), jnp.float32)
    window_factor = centred(streams_of[2], (STEPS, NB, STEPS, NB), (4 * NB) ** -0.5, 0.09375, ((1, 16), (3, 2)))
    inverse_t = draw_inverse_t(jax.random.fold_in(streams_of[5], 71), 0)
    trailing_factor = centred(streams_of[4], (ROWS, STEPS, NB), (STEPS * NB) ** -0.5, 0.09375, ((0, 16), (2, 2)))
    return {"right_side": right_side, "partial_in": partial_in, "window_factor": window_factor, "inverse_t": inverse_t, "trailing_factor": trailing_factor}


def reference(right_side, partial_in, window_factor, inverse_t, trailing_factor):
    solved_list = []
    for block in range(STEPS):
        fanned = jnp.sum(partial_in[:, block], axis=0)
        for prior in range(block):
            fanned = fanned + jnp.dot(window_factor[block, :, prior, :], solved_list[prior], preferred_element_type=jnp.float32)
        residue = (right_side[block].astype(jnp.float32) - fanned).astype(jnp.bfloat16)
        solution = jnp.dot(inverse_t[block].T, residue, preferred_element_type=jnp.float32)
        solved_list.append(solution.astype(jnp.bfloat16))
    solved = jnp.stack(solved_list)
    flat_factor = trailing_factor.reshape(ROWS, STEPS * NB)
    trailing = jnp.dot(flat_factor, solved.reshape(STEPS * NB, RHS), preferred_element_type=jnp.float32)
    return solved, trailing
```

```python
import functools

import jax
import jax.numpy as jnp
from jax import lax
from jax.experimental import pallas as pl
from jax.experimental.pallas import tpu as pltpu
from jax.sharding import PartitionSpec as P

MESH = pl.DeviceIdType.MESH
INNER = 4
F32 = jnp.float32
BF16 = jnp.bfloat16


def steps_over(count, first, body):
    if count - first <= 4:
        for step in range(first, count):
            body(step)
    else:
        lax.fori_loop(first, count, lambda step, c: (body(step), c)[1], 0)


class Place:
    def __init__(self, wide, narrow):
        self.outer_count, self.narrow_count = wide // INNER, narrow
        w, n = lax.axis_index("wide"), lax.axis_index("narrow")
        self.w, self.n = w, n
        self.z, self.r = lax.div(w, INNER), lax.rem(w, INNER)
        self.c = lax.rem(n, 2)
        one = self.r + 1 - 2 * lax.rem(self.r, 2)
        two = lax.rem(self.r + 2, INNER)
        self.ra = (1 - self.c) * one + self.c * two
        self.rb = self.c * one + (1 - self.c) * two
        self.rd = INNER - 1 - self.r

    def outer(self, shift):
        return lax.rem(self.z + shift + self.outer_count, self.outer_count)

    def at(self, z, r):
        return (z * INNER + r, self.n)

    def side(self, shift):
        return lax.rem(self.n + shift + self.narrow_count, self.narrow_count)


class Gather:
    def __init__(self, place, buf, sems, k, h, peers, needed=None):
        self.p, self.buf, self.k, self.h, self.peers = place, buf, k, h, peers
        self.zs, self.zr, self.as_, self.ar, self.bs, self.br, self.ds, self.dr = sems
        self.needed = needed

    def when(self, h, z, body):
        if self.needed is None:
            body()
        else:
            pl.when(self.needed(h, z))(body)

    def copy(self, z, r, send, recv, device):
        ref = self.buf.at[self.k, self.h, z, r]
        return pltpu.make_async_remote_copy(
            src_ref=ref, dst_ref=ref, send_sem=send, recv_sem=recv, device_id=device, device_id_type=MESH
        )

    def z_copy(self, d, z, to):
        return self.copy(z, self.p.r, self.zs.at[d], self.zr.at[self.k, d], self.p.at(to, self.p.r))

    def a_copy(self, d, z, r):
        return self.copy(z, r, self.as_.at[d], self.ar.at[self.k, d], self.p.at(self.p.z, self.p.ra))

    def b_copy(self, d, which, z, r):
        return self.copy(z, r, self.bs.at[which, d], self.br.at[self.k, which, d], self.p.at(self.p.z, self.p.rb))

    def d_copy(self, d, i, z, h, to):
        ref = self.buf.at[self.k, h, z]
        return pltpu.make_async_remote_copy(
            src_ref=ref, dst_ref=ref, send_sem=self.ds.at[i, d], recv_sem=self.dr.at[self.k, i, d],
            device_id=(self.p.w, to), device_id_type=MESH,
        )

    def own(self):
        p = self.p

        def go():
            steps_over(p.outer_count, 1, lambda d: self.z_copy(d, p.z, p.outer(d)).start())
            self.a_copy(0, p.z, p.r).start()
            self.b_copy(0, 0, p.z, p.r).start()

        self.when(self.h, p.z, go)

    def line(self):
        p = self.p

        def one(d):
            z = p.outer(-d)

            def go():
                self.z_copy(d, z, p.z).wait_recv()
                self.a_copy(d, z, p.r).start()
                self.b_copy(d, 0, z, p.r).start()

            self.when(self.h, z, go)

        steps_over(p.outer_count, 1, one)

    def first_side(self):
        p = self.p

        def one(d):
            z = p.outer(-d)

            def go():
                self.a_copy(d, z, p.ra).wait_recv()
                self.b_copy(d, 1, z, p.ra).start()

            self.when(self.h, z, go)

        steps_over(p.outer_count, 0, one)

    def second_side(self):
        p = self.p

        def one(d):
            z = p.outer(-d)

            def go():
                self.b_copy(d, 0, z, p.rb).wait_recv()
                self.b_copy(d, 1, z, p.rd).wait_recv()
                for i, (to, _) in enumerate(self.peers):
                    self.d_copy(d, i, z, self.h, to).start()

            self.when(self.h, z, go)

        steps_over(p.outer_count, 0, one)

    def across(self):
        p = self.p
        for i, (_, source) in enumerate(self.peers):

            def one(d, i=i, source=source):
                z = p.outer(-d)
                self.when(source, z, lambda: self.d_copy(d, i, z, source, p.n).wait_recv())

            steps_over(p.outer_count, 0, one)

    def sent(self):
        p = self.p
        self.when(
            self.h, p.z,
            lambda: steps_over(p.outer_count, 1, lambda d: self.z_copy(d, p.z, p.outer(d)).wait_send()),
        )

        def one(d):
            z = p.outer(-d)

            def go():
                self.a_copy(d, z, p.r).wait_send()
                self.b_copy(d, 0, z, p.r).wait_send()
                self.b_copy(d, 1, z, p.ra).wait_send()
                for i, (to, _) in enumerate(self.peers):
                    self.d_copy(d, i, z, self.h, to).wait_send()

            self.when(self.h, z, go)

        steps_over(p.outer_count, 0, one)


def kernel(
    wide, narrow, right, partial, window, inverse, factor, solved, trailing,
    ybuf, ibuf, xbuf, tbuf, pbuf, wbuf, fan,
    y_zs, y_zr, y_as, y_ar, y_bs, y_br, y_ds, y_dr,
    i_zs, i_zr, i_as, i_ar, i_bs, i_br, i_ds, i_dr,
    p_s, p_r, w_s, w_r, t_s, t_r, t_own,
):
    place = Place(wide, narrow)
    n = place.n
    blocks, rows, rhs = right.shape
    cols = inverse.shape[2]
    half = rhs // 2
    step_rows = wide * rows
    outer_rows = INNER * rows
    trail = trailing.shape[0]
    shifts = range(1, narrow)

    barrier = pltpu.get_barrier_semaphore()

    def greet(device):
        pl.semaphore_signal(barrier, inc=1, device_id=device, device_id_type=MESH)

    steps_over(place.outer_count, 1, lambda d: greet(place.at(place.outer(d), place.r)))
    greet(place.at(place.z, place.ra))
    greet(place.at(place.z, place.rb))
    for s in shifts:
        greet((place.w, place.side(s)))
    pl.semaphore_wait(barrier, place.outer_count - 1 + 2 + narrow - 1)

    def side_copy(src, dst, send, recv, s):
        return pltpu.make_async_remote_copy(
            src_ref=src, dst_ref=dst, send_sem=send, recv_sem=recv,
            device_id=(place.w, place.side(s)), device_id_type=MESH,
        )

    def p_copy(s, k):
        return side_copy(partial.at[0, k], pbuf.at[s - 1, k], p_s.at[s - 1, k], p_r.at[s - 1, k], s)

    def w_copy(s, slot):
        return side_copy(window, wbuf.at[slot], w_s.at[s - 1], w_r.at[s - 1], s)

    def t_copy(s, slot):
        to = place.side(s)
        return side_copy(
            factor.at[:, pl.ds(pl.multiple_of(to * trail, trail), trail), :], tbuf.at[slot],
            t_s.at[s - 1], t_r.at[s - 1], s,
        )

    t_here = pltpu.make_async_copy(
        factor.at[:, pl.ds(pl.multiple_of(n * trail, trail), trail), :], tbuf.at[n], t_own
    )

    for s in shifts:
        p_copy(s, 0).start()

    mate = n + 1 - 2 * place.c
    y_sems = (y_zs, y_zr, y_as, y_ar, y_bs, y_br, y_ds, y_dr)
    i_sems = (i_zs, i_zr, i_as, i_ar, i_bs, i_br, i_ds, i_dr)
    everyone = [(place.side(s), place.side(-s)) for s in shifts]
    ys = [Gather(place, ybuf, y_sems, k, place.c, [(mate, 1 - place.c)]) for k in range(blocks)]
    needed = lambda h, z: z * outer_rows < (h + 1) * cols
    inv = [Gather(place, ibuf, i_sems, k, n, everyone, needed) for k in range(blocks)]

    ibuf[0, n, place.z, place.r] = inverse[0]
    inv[0].own()

    def residue(k):
        fanned = partial[0, k]
        for s in shifts:
            fanned = fanned + pbuf[s - 1, k]
        if k > 0:
            fanned = fanned + fan[...]
        value = (right[k].astype(F32) - fanned).astype(BF16)
        for c in range(2):

            @pl.when(place.c == c)
            def _():
                ybuf[k, c, place.z, place.r] = value[:, c * half:(c + 1) * half]

    for s in shifts:
        p_copy(s, 0).wait_recv()
    residue(0)
    ys[0].own()

    for s in shifts:
        for k in range(1, blocks):
            p_copy(s, k).start()
        w_copy(s, n).start()
        t_copy(s, n).start()
    t_here.start()
    for k in range(1, blocks):
        ibuf[k, n, place.z, place.r] = inverse[k]
    wbuf[n] = window[...]

    width = min(256, cols)

    def solve(k):
        for h in range(narrow):
            deep = min(place.outer_count, -(-(h + 1) * cols // outer_rows))

            def tile(t, h=h, deep=deep):
                at = pl.multiple_of(t * width, width)
                lhs = ibuf[k, h, :deep, :, :, pl.ds(at, width)].reshape(deep * outer_rows, width)
                for c in range(2):
                    rhs_part = ybuf[k, c, :deep].reshape(deep * outer_rows, half)
                    out = lax.dot_general(lhs, rhs_part, (((0,), (0,)), ((), ())), preferred_element_type=F32)
                    xbuf[k, pl.ds(pl.multiple_of(h * cols + at, width), width), c * half:(c + 1) * half] = out.astype(BF16)

            lax.fori_loop(0, cols // width, lambda t, carry: (tile(t), carry)[1], 0)

    def fan_in(k, j):
        total = None
        for h in range(narrow):
            term = jnp.dot(
                wbuf[h, k * (k - 1) // 2 + j], xbuf[j, h * cols:(h + 1) * cols, :], preferred_element_type=F32
            )
            total = term if total is None else total + term
        if j == 0:
            fan[...] = total
        else:
            fan[...] += total

    high = min(256, trail)

    def trail_in(k):
        def tile(t):
            at = pl.ds(pl.multiple_of(t * high, high), high)
            total = None
            for h in range(narrow):
                term = jnp.dot(tbuf[h, k, at, :], xbuf[k, h * cols:(h + 1) * cols, :], preferred_element_type=F32)
                total = term if total is None else total + term
            if k == 0:
                trailing[at, :] = total
            else:
                trailing[at, :] += total

        lax.fori_loop(0, trail // high, lambda t, carry: (tile(t), carry)[1], 0)

    inv[0].line()
    ys[0].line()
    for k in range(blocks):
        y, last = ys[k], k == blocks - 1
        if k > 0:
            y.line()
        y.first_side()
        if k == 0:
            inv[0].first_side()
        if not last:
            if k > 0:
                inv[k].sent()
        if k == 0:
            inv[0].second_side()
            inv[0].sent()
        if not last:
            inv[k + 1].own()
        if k == 1:
            for s in shifts:
                t_copy(s, place.side(-s)).wait_recv()
            t_here.wait()
        if k > 0:
            trail_in(k - 1)
            if not last:
                for j in range(k):
                    fan_in(k + 1, j)
        y.second_side()
        if not last:
            inv[k + 1].line()
        inv[k].across()
        y.across()
        solve(k)
        y.sent()
        if not last:
            if k == 0:
                for s in shifts:
                    w_copy(s, place.side(-s)).wait_recv()
                    for later in range(1, blocks):
                        p_copy(s, later).wait_recv()
            fan_in(k + 1, k)
            residue(k + 1)
            ys[k + 1].own()
            inv[k + 1].first_side()
            inv[k + 1].second_side()
    inv[blocks - 1].sent()
    trail_in(blocks - 1)
    for h in range(narrow):

        @pl.when(n == h)
        def _():
            for k in range(blocks):
                solved[k] = xbuf[k, h * cols:(h + 1) * cols, :]

    for s in shifts:
        for k in range(blocks):
            p_copy(s, k).wait_send()
        w_copy(s, n).wait_send()
        t_copy(s, n).wait_send()


def per_device(wide, narrow, right_side, partial_in, window_factor, inverse_t, trailing_factor):
    blocks, rows, rhs = right_side.shape
    cols = inverse_t.shape[2]
    trail = trailing_factor.shape[0] // narrow
    outer = wide // INNER
    window = jnp.stack([window_factor[k, :, j, :] for k in range(blocks) for j in range(k)])
    factor = jnp.transpose(trailing_factor, (1, 0, 2))
    dma = pltpu.SemaphoreType.DMA

    def gather_sems(peers):
        return [
            dma((outer,)), dma((blocks, outer)),
            dma((outer,)), dma((blocks, outer)),
            dma((2, outer)), dma((blocks, 2, outer)),
            dma((peers, outer)), dma((blocks, peers, outer)),
        ]

    vmem = pl.BlockSpec(memory_space=pltpu.VMEM)
    step_rows = wide * rows
    return pl.pallas_call(
        functools.partial(kernel, wide, narrow),
        out_shape=(
            jax.ShapeDtypeStruct((blocks, cols, rhs), BF16),
            jax.ShapeDtypeStruct((trail, rhs), F32),
        ),
        in_specs=[vmem, vmem, vmem, vmem, pl.BlockSpec(memory_space=pl.ANY)],
        out_specs=(vmem, vmem),
        scratch_shapes=[
            pltpu.VMEM((blocks, 2, outer, INNER, rows, rhs // 2), BF16),
            pltpu.VMEM((blocks, narrow, outer, INNER, rows, cols), BF16),
            pltpu.VMEM((blocks, step_rows, rhs), BF16),
            pltpu.VMEM((narrow, blocks, trail, cols), BF16),
            pltpu.VMEM((narrow - 1, blocks, rows, rhs), F32),
            pltpu.VMEM((narrow, blocks * (blocks - 1) // 2, rows, cols), BF16),
            pltpu.VMEM((rows, rhs), F32),
            *gather_sems(1),
            *gather_sems(narrow - 1),
            dma((narrow - 1, blocks)), dma((narrow - 1, blocks)),
            dma((narrow - 1,)), dma((narrow - 1,)),
            dma((narrow - 1,)), dma((narrow - 1,)),
            dma,
        ],
        compiler_params=pltpu.CompilerParams(
            collective_id=0, has_side_effects=True, vmem_limit_bytes=56 * 1024 * 1024
        ),
    )(right_side, partial_in, window, inverse_t, factor)


def solution(mesh):
    placed = (
        P(None, "wide", None),
        P("narrow", None, "wide", None),
        P(None, "wide", None, "narrow"),
        P(None, "wide", "narrow"),
        P("wide", None, "narrow"),
    )
    return jax.shard_map(
        functools.partial(per_device, mesh.shape["wide"], mesh.shape["narrow"]),
        mesh=mesh,
        in_specs=placed,
        out_specs=(P(None, "narrow", None), P(("wide", "narrow"), None)),
        check_vma=False,
    )
```

```python
import functools

import jax
import jax.numpy as jnp
from jax import lax
from jax.experimental import pallas as pl
from jax.experimental.pallas import tpu as pltpu
from jax.sharding import PartitionSpec as P

MESH = pl.DeviceIdType.MESH
INNER = 4
F32 = jnp.float32
BF16 = jnp.bfloat16


def steps_over(count, first, body):
    if count - first <= 4:
        for step in range(first, count):
            body(step)
    else:
        lax.fori_loop(first, count, lambda step, c: (body(step), c)[1], 0)


class Place:
    def __init__(self, wide, narrow):
        self.outer_count, self.narrow_count = wide // INNER, narrow
        w, n = lax.axis_index("wide"), lax.axis_index("narrow")
        self.w, self.n = w, n
        self.z, self.r = lax.div(w, INNER), lax.rem(w, INNER)
        self.c = lax.rem(n, 2)
        one = self.r + 1 - 2 * lax.rem(self.r, 2)
        two = lax.rem(self.r + 2, INNER)
        self.ra = (1 - self.c) * one + self.c * two
        self.rb = self.c * one + (1 - self.c) * two
        self.rd = INNER - 1 - self.r

    def outer(self, shift):
        return lax.rem(self.z + shift + self.outer_count, self.outer_count)

    def at(self, z, r):
        return (z * INNER + r, self.n)

    def side(self, shift):
        return lax.rem(self.n + shift + self.narrow_count, self.narrow_count)


class Gather:
    def __init__(self, place, buf, sems, k, h, peers, needed=None):
        self.p, self.buf, self.k, self.h, self.peers = place, buf, k, h, peers
        self.zs, self.zr, self.as_, self.ar, self.bs, self.br, self.ds, self.dr = sems
        self.needed = needed

    def when(self, h, z, body):
        if self.needed is None:
            body()
        else:
            pl.when(self.needed(h, z))(body)

    def copy(self, z, r, send, recv, device):
        ref = self.buf.at[self.k, self.h, z, r]
        return pltpu.make_async_remote_copy(
            src_ref=ref, dst_ref=ref, send_sem=send, recv_sem=recv, device_id=device, device_id_type=MESH
        )

    def z_copy(self, d, z, to):
        return self.copy(z, self.p.r, self.zs.at[self.k % 2, d], self.zr.at[self.k, d], self.p.at(to, self.p.r))

    def a_copy(self, d, z, r):
        return self.copy(z, r, self.as_.at[self.k % 2, d], self.ar.at[self.k, d], self.p.at(self.p.z, self.p.ra))

    def b_copy(self, d, which, z, r):
        return self.copy(z, r, self.bs.at[self.k % 2, which, d], self.br.at[self.k, which, d], self.p.at(self.p.z, self.p.rb))

    def d_copy(self, d, i, z, h, to):
        ref = self.buf.at[self.k, h, z]
        return pltpu.make_async_remote_copy(
            src_ref=ref, dst_ref=ref, send_sem=self.ds.at[self.k % 2, i, d], recv_sem=self.dr.at[self.k, i, d],
            device_id=(self.p.w, to), device_id_type=MESH,
        )

    def own(self):
        p = self.p

        def go():
            steps_over(p.outer_count, 1, lambda d: self.z_copy(d, p.z, p.outer(d)).start())
            self.a_copy(0, p.z, p.r).start()
            self.b_copy(0, 0, p.z, p.r).start()

        self.when(self.h, p.z, go)

    def line(self):
        p = self.p

        def one(d):
            z = p.outer(-d)

            def go():
                self.z_copy(d, z, p.z).wait_recv()
                self.a_copy(d, z, p.r).start()
                self.b_copy(d, 0, z, p.r).start()

            self.when(self.h, z, go)

        steps_over(p.outer_count, 1, one)

    def first_side(self):
        p = self.p

        def one(d):
            z = p.outer(-d)

            def go():
                self.a_copy(d, z, p.ra).wait_recv()
                self.b_copy(d, 1, z, p.ra).start()

            self.when(self.h, z, go)

        steps_over(p.outer_count, 0, one)

    def second_side(self):
        p = self.p

        def one(d):
            z = p.outer(-d)

            def go():
                self.b_copy(d, 0, z, p.rb).wait_recv()
                self.b_copy(d, 1, z, p.rd).wait_recv()
                for i, (to, _) in enumerate(self.peers):
                    self.d_copy(d, i, z, self.h, to).start()

            self.when(self.h, z, go)

        steps_over(p.outer_count, 0, one)

    def across(self):
        p = self.p
        for i, (_, source) in enumerate(self.peers):

            def one(d, i=i, source=source):
                z = p.outer(-d)
                self.when(source, z, lambda: self.d_copy(d, i, z, source, p.n).wait_recv())

            steps_over(p.outer_count, 0, one)

    def sent(self):
        p = self.p
        self.when(
            self.h, p.z,
            lambda: steps_over(p.outer_count, 1, lambda d: self.z_copy(d, p.z, p.outer(d)).wait_send()),
        )

        def one(d):
            z = p.outer(-d)

            def go():
                self.a_copy(d, z, p.r).wait_send()
                self.b_copy(d, 0, z, p.r).wait_send()
                self.b_copy(d, 1, z, p.ra).wait_send()
                for i, (to, _) in enumerate(self.peers):
                    self.d_copy(d, i, z, self.h, to).wait_send()

            self.when(self.h, z, go)

        steps_over(p.outer_count, 0, one)


def kernel(
    wide, narrow, right, partial, window, inverse, factor, solved, trailing,
    ybuf, ibuf, xbuf, tbuf, pbuf, wbuf, fan,
    y_zs, y_zr, y_as, y_ar, y_bs, y_br, y_ds, y_dr,
    i_zs, i_zr, i_as, i_ar, i_bs, i_br, i_ds, i_dr,
    p_s, p_r, w_s, w_r, t_s, t_r, t_own,
):
    place = Place(wide, narrow)
    n = place.n
    blocks, rows, rhs = right.shape
    cols = inverse.shape[2]
    half = rhs // 2
    step_rows = wide * rows
    outer_rows = INNER * rows
    trail = trailing.shape[0]
    shifts = range(1, narrow)

    barrier = pltpu.get_barrier_semaphore()

    def greet(device):
        pl.semaphore_signal(barrier, inc=1, device_id=device, device_id_type=MESH)

    steps_over(place.outer_count, 1, lambda d: greet(place.at(place.outer(d), place.r)))
    greet(place.at(place.z, place.ra))
    greet(place.at(place.z, place.rb))
    for s in shifts:
        greet((place.w, place.side(s)))
    pl.semaphore_wait(barrier, place.outer_count - 1 + 2 + narrow - 1)

    def side_copy(src, dst, send, recv, s):
        return pltpu.make_async_remote_copy(
            src_ref=src, dst_ref=dst, send_sem=send, recv_sem=recv,
            device_id=(place.w, place.side(s)), device_id_type=MESH,
        )

    def p_copy(s, k):
        return side_copy(partial.at[0, k], pbuf.at[s - 1, k], p_s.at[s - 1, k], p_r.at[s - 1, k], s)

    def w_copy(s, slot):
        return side_copy(window, wbuf.at[slot], w_s.at[s - 1], w_r.at[s - 1], s)

    def t_copy(s, slot):
        to = place.side(s)
        return side_copy(
            factor.at[:, pl.ds(pl.multiple_of(to * trail, trail), trail), :], tbuf.at[slot],
            t_s.at[s - 1], t_r.at[s - 1], s,
        )

    t_here = pltpu.make_async_copy(
        factor.at[:, pl.ds(pl.multiple_of(n * trail, trail), trail), :], tbuf.at[n], t_own
    )

    for s in shifts:
        p_copy(s, 0).start()

    mate = n + 1 - 2 * place.c
    y_sems = (y_zs, y_zr, y_as, y_ar, y_bs, y_br, y_ds, y_dr)
    i_sems = (i_zs, i_zr, i_as, i_ar, i_bs, i_br, i_ds, i_dr)
    everyone = [(place.side(s), place.side(-s)) for s in shifts]
    ys = [Gather(place, ybuf, y_sems, k, place.c, [(mate, 1 - place.c)]) for k in range(blocks)]
    needed = lambda h, z: z * outer_rows < (h + 1) * cols
    inv = [Gather(place, ibuf, i_sems, k, n, everyone, needed) for k in range(blocks)]

    ibuf[0, n, place.z, place.r] = inverse[0]
    inv[0].own()

    def residue(k):
        fanned = partial[0, k]
        for s in shifts:
            fanned = fanned + pbuf[s - 1, k]
        if k > 0:
            fanned = fanned + fan[...]
        value = (right[k].astype(F32) - fanned).astype(BF16)
        for c in range(2):

            @pl.when(place.c == c)
            def _():
                ybuf[k, c, place.z, place.r] = value[:, c * half:(c + 1) * half]

    for s in shifts:
        p_copy(s, 0).wait_recv()
    residue(0)
    ys[0].own()

    for s in shifts:
        for k in range(1, blocks):
            p_copy(s, k).start()
        w_copy(s, n).start()
        t_copy(s, n).start()
    t_here.start()
    for k in range(1, blocks):
        ibuf[k, n, place.z, place.r] = inverse[k]
    wbuf[n] = window[...]

    width = min(256, cols)

    def solve(k):
        for h in range(narrow):
            deep = min(place.outer_count, -(-(h + 1) * cols // outer_rows))

            def tile(t, h=h, deep=deep):
                at = pl.multiple_of(t * width, width)
                lhs = ibuf[k, h, :deep, :, :, pl.ds(at, width)].reshape(deep * outer_rows, width)
                for c in range(2):
                    rhs_part = ybuf[k, c, :deep].reshape(deep * outer_rows, half)
                    out = lax.dot_general(lhs, rhs_part, (((0,), (0,)), ((), ())), preferred_element_type=F32)
                    xbuf[k, pl.ds(pl.multiple_of(h * cols + at, width), width), c * half:(c + 1) * half] = out.astype(BF16)

            lax.fori_loop(0, cols // width, lambda t, carry: (tile(t), carry)[1], 0)

    def fan_in(k, j):
        total = None
        for h in range(narrow):
            term = jnp.dot(
                wbuf[h, k * (k - 1) // 2 + j], xbuf[j, h * cols:(h + 1) * cols, :], preferred_element_type=F32
            )
            total = term if total is None else total + term
        if j == 0:
            fan[...] = total
        else:
            fan[...] += total

    high = min(256, trail)

    def trail_in(k):
        def tile(t):
            at = pl.ds(pl.multiple_of(t * high, high), high)
            total = None
            for h in range(narrow):
                term = jnp.dot(tbuf[h, k, at, :], xbuf[k, h * cols:(h + 1) * cols, :], preferred_element_type=F32)
                total = term if total is None else total + term
            if k == 0:
                trailing[at, :] = total
            else:
                trailing[at, :] += total

        lax.fori_loop(0, trail // high, lambda t, carry: (tile(t), carry)[1], 0)

    if blocks > 1:
        inv[1].own()
    inv[0].line()
    ys[0].line()
    inv[0].first_side()
    for k in range(blocks):
        y, last = ys[k], k == blocks - 1
        if k > 0:
            y.line()
        y.first_side()
        if k == 0:
            inv[0].second_side()
            if not last:
                inv[1].line()
        if not last:
            inv[k + 1].first_side()
        if k + 2 < blocks:
            inv[k].sent()
            inv[k + 2].own()
        if k == 1:
            for s in shifts:
                t_copy(s, place.side(-s)).wait_recv()
            t_here.wait()
        if k > 0:
            trail_in(k - 1)
            if not last:
                for j in range(k):
                    fan_in(k + 1, j)
        y.second_side()
        inv[k].across()
        y.across()
        solve(k)
        y.sent()
        if not last:
            if k == 0:
                for s in shifts:
                    w_copy(s, place.side(-s)).wait_recv()
                    for later in range(1, blocks):
                        p_copy(s, later).wait_recv()
            fan_in(k + 1, k)
            residue(k + 1)
            ys[k + 1].own()
            inv[k + 1].second_side()
        if k + 2 < blocks:
            inv[k + 2].line()
    for k in range(max(0, blocks - 2), blocks):
        inv[k].sent()
    trail_in(blocks - 1)
    for h in range(narrow):

        @pl.when(n == h)
        def _():
            for k in range(blocks):
                solved[k] = xbuf[k, h * cols:(h + 1) * cols, :]

    for s in shifts:
        for k in range(blocks):
            p_copy(s, k).wait_send()
        w_copy(s, n).wait_send()
        t_copy(s, n).wait_send()


def per_device(wide, narrow, right_side, partial_in, window_factor, inverse_t, trailing_factor):
    blocks, rows, rhs = right_side.shape
    cols = inverse_t.shape[2]
    trail = trailing_factor.shape[0] // narrow
    outer = wide // INNER
    window = jnp.stack([window_factor[k, :, j, :] for k in range(blocks) for j in range(k)])
    factor = jnp.transpose(trailing_factor, (1, 0, 2))
    dma = pltpu.SemaphoreType.DMA

    def gather_sems(peers):
        return [
            dma((2, outer)), dma((blocks, outer)),
            dma((2, outer)), dma((blocks, outer)),
            dma((2, 2, outer)), dma((blocks, 2, outer)),
            dma((2, peers, outer)), dma((blocks, peers, outer)),
        ]

    vmem = pl.BlockSpec(memory_space=pltpu.VMEM)
    step_rows = wide * rows
    return pl.pallas_call(
        functools.partial(kernel, wide, narrow),
        out_shape=(
            jax.ShapeDtypeStruct((blocks, cols, rhs), BF16),
            jax.ShapeDtypeStruct((trail, rhs), F32),
        ),
        in_specs=[vmem, vmem, vmem, vmem, pl.BlockSpec(memory_space=pl.ANY)],
        out_specs=(vmem, vmem),
        scratch_shapes=[
            pltpu.VMEM((blocks, 2, outer, INNER, rows, rhs // 2), BF16),
            pltpu.VMEM((blocks, narrow, outer, INNER, rows, cols), BF16),
            pltpu.VMEM((blocks, step_rows, rhs), BF16),
            pltpu.VMEM((narrow, blocks, trail, cols), BF16),
            pltpu.VMEM((narrow - 1, blocks, rows, rhs), F32),
            pltpu.VMEM((narrow, blocks * (blocks - 1) // 2, rows, cols), BF16),
            pltpu.VMEM((rows, rhs), F32),
            *gather_sems(1),
            *gather_sems(narrow - 1),
            dma((narrow - 1, blocks)), dma((narrow - 1, blocks)),
            dma((narrow - 1,)), dma((narrow - 1,)),
            dma((narrow - 1,)), dma((narrow - 1,)),
            dma,
        ],
        compiler_params=pltpu.CompilerParams(
            collective_id=0, has_side_effects=True, vmem_limit_bytes=56 * 1024 * 1024
        ),
    )(right_side, partial_in, window, inverse_t, factor)


def solution(mesh):
    placed = (
        P(None, "wide", None),
        P("narrow", None, "wide", None),
        P(None, "wide", None, "narrow"),
        P(None, "wide", "narrow"),
        P("wide", None, "narrow"),
    )
    return jax.shard_map(
        functools.partial(per_device, mesh.shape["wide"], mesh.shape["narrow"]),
        mesh=mesh,
        in_specs=placed,
        out_specs=(P(None, "narrow", None), P(("wide", "narrow"), None)),
        check_vma=False,
    )
```

```python
import functools

import jax
import jax.numpy as jnp
from jax import lax
from jax.experimental import pallas as pl
from jax.experimental.pallas import tpu as pltpu
from jax.sharding import PartitionSpec as P

MESH = pl.DeviceIdType.MESH
INNER = 4
F32 = jnp.float32
BF16 = jnp.bfloat16


def steps_over(count, first, body):
    if count - first <= 4:
        for step in range(first, count):
            body(step)
    else:
        lax.fori_loop(first, count, lambda step, c: (body(step), c)[1], 0)


class Place:
    def __init__(self, wide, narrow):
        self.outer_count, self.narrow_count = wide // INNER, narrow
        w, n = lax.axis_index("wide"), lax.axis_index("narrow")
        self.w, self.n = w, n
        self.z, self.r = lax.div(w, INNER), lax.rem(w, INNER)
        self.c = lax.rem(n, 2)
        one = self.r + 1 - 2 * lax.rem(self.r, 2)
        two = lax.rem(self.r + 2, INNER)
        self.ra = (1 - self.c) * one + self.c * two
        self.rb = self.c * one + (1 - self.c) * two
        self.rd = INNER - 1 - self.r

    def outer(self, shift):
        return lax.rem(self.z + shift + self.outer_count, self.outer_count)

    def at(self, z, r):
        return (z * INNER + r, self.n)

    def side(self, shift):
        return lax.rem(self.n + shift + self.narrow_count, self.narrow_count)


class Gather:
    def __init__(self, place, buf, sems, k, h, peers, needed=None):
        self.p, self.buf, self.k, self.h, self.peers = place, buf, k, h, peers
        self.zs, self.zr, self.as_, self.ar, self.bs, self.br, self.ds, self.dr = sems
        self.needed = needed

    def when(self, h, z, body):
        if self.needed is None:
            body()
        else:
            pl.when(self.needed(h, z))(body)

    def copy(self, z, r, send, recv, device):
        ref = self.buf.at[self.k, self.h, z, r]
        return pltpu.make_async_remote_copy(
            src_ref=ref, dst_ref=ref, send_sem=send, recv_sem=recv, device_id=device, device_id_type=MESH
        )

    def z_copy(self, d, z, to):
        return self.copy(z, self.p.r, self.zs.at[self.k % 2, d], self.zr.at[self.k, d], self.p.at(to, self.p.r))

    def a_copy(self, d, z, r):
        return self.copy(z, r, self.as_.at[self.k % 2, d], self.ar.at[self.k, d], self.p.at(self.p.z, self.p.ra))

    def b_copy(self, d, which, z, r):
        return self.copy(z, r, self.bs.at[self.k % 2, which, d], self.br.at[self.k, which, d], self.p.at(self.p.z, self.p.rb))

    def d_copy(self, d, i, z, h, to):
        ref = self.buf.at[self.k, h, z]
        return pltpu.make_async_remote_copy(
            src_ref=ref, dst_ref=ref, send_sem=self.ds.at[self.k % 2, i, d], recv_sem=self.dr.at[self.k, i, d],
            device_id=(self.p.w, to), device_id_type=MESH,
        )

    def own(self):
        p = self.p

        def go():
            steps_over(p.outer_count, 1, lambda d: self.z_copy(d, p.z, p.outer(d)).start())
            self.a_copy(0, p.z, p.r).start()
            self.b_copy(0, 0, p.z, p.r).start()

        self.when(self.h, p.z, go)

    def line(self):
        p = self.p

        def one(d):
            z = p.outer(-d)

            def go():
                self.z_copy(d, z, p.z).wait_recv()
                self.a_copy(d, z, p.r).start()
                self.b_copy(d, 0, z, p.r).start()

            self.when(self.h, z, go)

        steps_over(p.outer_count, 1, one)

    def first_side(self):
        p = self.p

        def one(d):
            z = p.outer(-d)

            def go():
                self.a_copy(d, z, p.ra).wait_recv()
                self.b_copy(d, 1, z, p.ra).start()

            self.when(self.h, z, go)

        steps_over(p.outer_count, 0, one)

    def second_side(self):
        p = self.p

        def one(d):
            z = p.outer(-d)

            def go():
                self.b_copy(d, 0, z, p.rb).wait_recv()
                self.b_copy(d, 1, z, p.rd).wait_recv()
                for i, (to, _) in enumerate(self.peers):
                    self.d_copy(d, i, z, self.h, to).start()

            self.when(self.h, z, go)

        steps_over(p.outer_count, 0, one)

    def across(self):
        p = self.p
        for i, (_, source) in enumerate(self.peers):

            def one(d, i=i, source=source):
                z = p.outer(-d)
                self.when(source, z, lambda: self.d_copy(d, i, z, source, p.n).wait_recv())

            steps_over(p.outer_count, 0, one)

    def sent(self):
        p = self.p
        self.when(
            self.h, p.z,
            lambda: steps_over(p.outer_count, 1, lambda d: self.z_copy(d, p.z, p.outer(d)).wait_send()),
        )

        def one(d):
            z = p.outer(-d)

            def go():
                self.a_copy(d, z, p.r).wait_send()
                self.b_copy(d, 0, z, p.r).wait_send()
                self.b_copy(d, 1, z, p.ra).wait_send()
                for i, (to, _) in enumerate(self.peers):
                    self.d_copy(d, i, z, self.h, to).wait_send()

            self.when(self.h, z, go)

        steps_over(p.outer_count, 0, one)


def kernel(
    wide, narrow, right, partial, window, inverse, factor, solved, trailing,
    ybuf, ibuf, xbuf, tbuf, pbuf, wbuf, fan, turned,
    y_zs, y_zr, y_as, y_ar, y_bs, y_br, y_ds, y_dr,
    i_zs, i_zr, i_as, i_ar, i_bs, i_br, i_ds, i_dr,
    p_s, p_r, w_s, w_r, t_s, t_r, t_own,
):
    place = Place(wide, narrow)
    n = place.n
    blocks, rows, rhs = right.shape
    cols = inverse.shape[2]
    half = rhs // 2
    step_rows = wide * rows
    outer_rows = INNER * rows
    trail = trailing.shape[0]
    shifts = range(1, narrow)

    barrier = pltpu.get_barrier_semaphore()

    def greet(device):
        pl.semaphore_signal(barrier, inc=1, device_id=device, device_id_type=MESH)

    steps_over(place.outer_count, 1, lambda d: greet(place.at(place.outer(d), place.r)))
    greet(place.at(place.z, place.ra))
    greet(place.at(place.z, place.rb))
    for s in shifts:
        greet((place.w, place.side(s)))
    pl.semaphore_wait(barrier, place.outer_count - 1 + 2 + narrow - 1)

    def side_copy(src, dst, send, recv, s):
        return pltpu.make_async_remote_copy(
            src_ref=src, dst_ref=dst, send_sem=send, recv_sem=recv,
            device_id=(place.w, place.side(s)), device_id_type=MESH,
        )

    def p_copy(s, k):
        return side_copy(partial.at[0, k], pbuf.at[s - 1, k], p_s.at[s - 1, k], p_r.at[s - 1, k], s)

    def w_copy(s, slot):
        return side_copy(window, wbuf.at[slot], w_s.at[s - 1], w_r.at[s - 1], s)

    def t_copy(s, slot, k):
        to = place.side(s)
        return side_copy(
            factor.at[k, pl.ds(pl.multiple_of(to * trail, trail), trail), :], tbuf.at[slot, k],
            t_s.at[s - 1, k], t_r.at[s - 1, k], s,
        )

    t_here = pltpu.make_async_copy(
        factor.at[:, pl.ds(pl.multiple_of(n * trail, trail), trail), :], tbuf.at[n], t_own
    )

    for s in shifts:
        p_copy(s, 0).start()

    mate = n + 1 - 2 * place.c
    y_sems = (y_zs, y_zr, y_as, y_ar, y_bs, y_br, y_ds, y_dr)
    i_sems = (i_zs, i_zr, i_as, i_ar, i_bs, i_br, i_ds, i_dr)
    everyone = [(place.side(s), place.side(-s)) for s in shifts]
    ys = [Gather(place, ybuf, y_sems, k, place.c, [(mate, 1 - place.c)]) for k in range(blocks)]
    needed = lambda h, z: z * outer_rows < (h + 1) * cols
    inv = [Gather(place, ibuf, i_sems, k, n, everyone, needed) for k in range(blocks)]

    ibuf[0, n, place.z, place.r] = inverse[0]
    inv[0].own()

    def residue(k):
        fanned = partial[0, k]
        for s in shifts:
            fanned = fanned + pbuf[s - 1, k]
        if k > 0:
            fanned = fanned + fan[...]
        value = (right[k].astype(F32) - fanned).astype(BF16)
        for c in range(2):

            @pl.when(place.c == c)
            def _():
                ybuf[k, c, place.z, place.r] = value[:, c * half:(c + 1) * half]

    for s in shifts:
        p_copy(s, 0).wait_recv()
    residue(0)
    ys[0].own()

    for s in shifts:
        for k in range(1, blocks):
            p_copy(s, k).start()
        w_copy(s, n).start()
    t_here.start()
    for k in range(1, blocks):
        ibuf[k, n, place.z, place.r] = inverse[k]
    wbuf[n] = window[...]

    width = min(256, cols)

    def turn(k):
        inv[k].across()
        for h in range(narrow):
            deep = min(place.outer_count, -(-(h + 1) * cols // outer_rows))
            for q in range(deep):
                for t in range(cols // width):
                    block = ibuf[k, h, q, :, :, t * width:(t + 1) * width].reshape(outer_rows, width)
                    turned[h * cols + t * width:h * cols + (t + 1) * width, q * outer_rows:(q + 1) * outer_rows] = block.T

    def solve(k):
        for h in range(narrow):
            deep = min(place.outer_count, -(-(h + 1) * cols // outer_rows))

            def tile(t, h=h, deep=deep):
                at = pl.ds(pl.multiple_of(h * cols + t * width, width), width)
                lhs = turned[at, :deep * outer_rows]
                for c in range(2):
                    rhs_part = ybuf[k, c, :deep].reshape(deep * outer_rows, half)
                    out = jnp.dot(lhs, rhs_part, preferred_element_type=F32)
                    xbuf[k, at, c * half:(c + 1) * half] = out.astype(BF16)

            lax.fori_loop(0, cols // width, lambda t, carry: (tile(t), carry)[1], 0)

    def fan_in(k, j):
        total = None
        for h in range(narrow):
            term = jnp.dot(
                wbuf[h, k * (k - 1) // 2 + j], xbuf[j, h * cols:(h + 1) * cols, :], preferred_element_type=F32
            )
            total = term if total is None else total + term
        if j == 0:
            fan[...] = total
        else:
            fan[...] += total

    high = min(256, trail)

    def trail_in(k):
        def tile(t):
            at = pl.ds(pl.multiple_of(t * high, high), high)
            total = None
            for h in range(narrow):
                term = jnp.dot(tbuf[h, k, at, :], xbuf[k, h * cols:(h + 1) * cols, :], preferred_element_type=F32)
                total = term if total is None else total + term
            if k == 0:
                trailing[at, :] = total
            else:
                trailing[at, :] += total

        lax.fori_loop(0, trail // high, lambda t, carry: (tile(t), carry)[1], 0)

    sending = [[k, k + 1] if k == 1 else [k + (k > 1)] if k + (k > 1) < blocks else [] for k in range(blocks)]
    if blocks > 1:
        inv[1].own()
    inv[0].line()
    ys[0].line()
    inv[0].first_side()
    for k in range(blocks):
        y, last = ys[k], k == blocks - 1
        if k > 0:
            y.line()
        y.first_side()
        if k == 0:
            inv[0].second_side()
            if not last:
                inv[1].line()
        if not last:
            inv[k + 1].first_side()
        if k + 2 < blocks:
            inv[k].sent()
            inv[k + 2].own()
        if k == 1:
            t_here.wait()
        if k > 0:
            for s in shifts:
                t_copy(s, place.side(-s), k - 1).wait_recv()
            trail_in(k - 1)
            if not last:
                for j in range(k):
                    fan_in(k + 1, j)
        if k > 0:
            turn(k)
        y.second_side()
        if k == 0:
            turn(k)
        y.across()
        for part in sending[k]:
            for s in shifts:
                t_copy(s, n, part).start()
        solve(k)
        y.sent()
        if not last:
            if k == 0:
                for s in shifts:
                    w_copy(s, place.side(-s)).wait_recv()
                    for later in range(1, blocks):
                        p_copy(s, later).wait_recv()
            fan_in(k + 1, k)
            residue(k + 1)
            ys[k + 1].own()
            inv[k + 1].second_side()
        if k + 2 < blocks:
            inv[k + 2].line()
    for k in range(max(0, blocks - 2), blocks):
        inv[k].sent()
    for s in shifts:
        t_copy(s, place.side(-s), blocks - 1).wait_recv()
    trail_in(blocks - 1)
    for h in range(narrow):

        @pl.when(n == h)
        def _():
            for k in range(blocks):
                solved[k] = xbuf[k, h * cols:(h + 1) * cols, :]

    for s in shifts:
        for k in range(blocks):
            p_copy(s, k).wait_send()
        w_copy(s, n).wait_send()
        for k in range(blocks):
            t_copy(s, n, k).wait_send()


def per_device(wide, narrow, right_side, partial_in, window_factor, inverse_t, trailing_factor):
    blocks, rows, rhs = right_side.shape
    cols = inverse_t.shape[2]
    trail = trailing_factor.shape[0] // narrow
    outer = wide // INNER
    window = jnp.stack([window_factor[k, :, j, :] for k in range(blocks) for j in range(k)])
    factor = jnp.transpose(trailing_factor, (1, 0, 2))
    dma = pltpu.SemaphoreType.DMA

    def gather_sems(peers):
        return [
            dma((2, outer)), dma((blocks, outer)),
            dma((2, outer)), dma((blocks, outer)),
            dma((2, 2, outer)), dma((blocks, 2, outer)),
            dma((2, peers, outer)), dma((blocks, peers, outer)),
        ]

    vmem = pl.BlockSpec(memory_space=pltpu.VMEM)
    step_rows = wide * rows
    return pl.pallas_call(
        functools.partial(kernel, wide, narrow),
        out_shape=(
            jax.ShapeDtypeStruct((blocks, cols, rhs), BF16),
            jax.ShapeDtypeStruct((trail, rhs), F32),
        ),
        in_specs=[vmem, vmem, vmem, vmem, pl.BlockSpec(memory_space=pl.ANY)],
        out_specs=(vmem, vmem),
        scratch_shapes=[
            pltpu.VMEM((blocks, 2, outer, INNER, rows, rhs // 2), BF16),
            pltpu.VMEM((blocks, narrow, outer, INNER, rows, cols), BF16),
            pltpu.VMEM((blocks, step_rows, rhs), BF16),
            pltpu.VMEM((narrow, blocks, trail, cols), BF16),
            pltpu.VMEM((narrow - 1, blocks, rows, rhs), F32),
            pltpu.VMEM((narrow, blocks * (blocks - 1) // 2, rows, cols), BF16),
            pltpu.VMEM((rows, rhs), F32),
            pltpu.VMEM((step_rows, step_rows), BF16),
            *gather_sems(1),
            *gather_sems(narrow - 1),
            dma((narrow - 1, blocks)), dma((narrow - 1, blocks)),
            dma((narrow - 1,)), dma((narrow - 1,)),
            dma((narrow - 1, blocks)), dma((narrow - 1, blocks)),
            dma,
        ],
        compiler_params=pltpu.CompilerParams(
            collective_id=0, has_side_effects=True, vmem_limit_bytes=56 * 1024 * 1024
        ),
    )(right_side, partial_in, window, inverse_t, factor)


def solution(mesh):
    placed = (
        P(None, "wide", None),
        P("narrow", None, "wide", None),
        P(None, "wide", None, "narrow"),
        P(None, "wide", "narrow"),
        P("wide", None, "narrow"),
    )
    return jax.shard_map(
        functools.partial(per_device, mesh.shape["wide"], mesh.shape["narrow"]),
        mesh=mesh,
        in_specs=placed,
        out_specs=(P(None, "narrow", None), P(("wide", "narrow"), None)),
        check_vma=False,
    )
```

```python
import functools

import jax
import jax.numpy as jnp
from jax import lax
from jax.experimental import pallas as pl
from jax.experimental.pallas import tpu as pltpu
from jax.sharding import PartitionSpec as P

MESH = pl.DeviceIdType.MESH
INNER = 4
F32 = jnp.float32
BF16 = jnp.bfloat16


def steps_over(count, first, body):
    if count - first <= 4:
        for step in range(first, count):
            body(step)
    else:
        lax.fori_loop(first, count, lambda step, c: (body(step), c)[1], 0)


class Place:
    def __init__(self, wide, narrow):
        self.outer_count, self.narrow_count = wide // INNER, narrow
        w, n = lax.axis_index("wide"), lax.axis_index("narrow")
        self.w, self.n = w, n
        self.z, self.r = lax.div(w, INNER), lax.rem(w, INNER)
        self.c = lax.rem(n, 2)
        one = self.r + 1 - 2 * lax.rem(self.r, 2)
        two = lax.rem(self.r + 2, INNER)
        self.ra = (1 - self.c) * one + self.c * two
        self.rb = self.c * one + (1 - self.c) * two
        self.rd = INNER - 1 - self.r

    def outer(self, shift):
        return lax.rem(self.z + shift + self.outer_count, self.outer_count)

    def at(self, z, r):
        return (z * INNER + r, self.n)

    def side(self, shift):
        return lax.rem(self.n + shift + self.narrow_count, self.narrow_count)


class Gather:
    def __init__(self, place, buf, sems, k, h, peers, needed=None):
        self.p, self.buf, self.k, self.h, self.peers = place, buf, k, h, peers
        self.zs, self.zr, self.as_, self.ar, self.bs, self.br, self.ds, self.dr = sems
        self.needed = needed

    def when(self, h, z, body):
        if self.needed is None:
            body()
        else:
            pl.when(self.needed(h, z))(body)

    def copy(self, z, r, send, recv, device):
        ref = self.buf.at[self.k, self.h, z, r]
        return pltpu.make_async_remote_copy(
            src_ref=ref, dst_ref=ref, send_sem=send, recv_sem=recv, device_id=device, device_id_type=MESH
        )

    def z_copy(self, d, z, to):
        return self.copy(z, self.p.r, self.zs.at[self.k % 2, d], self.zr.at[self.k, d], self.p.at(to, self.p.r))

    def a_copy(self, d, z, r):
        return self.copy(z, r, self.as_.at[self.k % 2, d], self.ar.at[self.k, d], self.p.at(self.p.z, self.p.ra))

    def b_copy(self, d, which, z, r):
        return self.copy(z, r, self.bs.at[self.k % 2, which, d], self.br.at[self.k, which, d], self.p.at(self.p.z, self.p.rb))

    def d_copy(self, d, i, z, h, to):
        ref = self.buf.at[self.k, h, z]
        return pltpu.make_async_remote_copy(
            src_ref=ref, dst_ref=ref, send_sem=self.ds.at[self.k % 2, i, d], recv_sem=self.dr.at[self.k, i, d],
            device_id=(self.p.w, to), device_id_type=MESH,
        )

    def own(self):
        p = self.p

        def go():
            steps_over(p.outer_count, 1, lambda d: self.z_copy(d, p.z, p.outer(d)).start())
            self.a_copy(0, p.z, p.r).start()
            self.b_copy(0, 0, p.z, p.r).start()

        self.when(self.h, p.z, go)

    def line(self):
        p = self.p

        def one(d):
            z = p.outer(-d)

            def go():
                self.z_copy(d, z, p.z).wait_recv()
                self.a_copy(d, z, p.r).start()
                self.b_copy(d, 0, z, p.r).start()

            self.when(self.h, z, go)

        steps_over(p.outer_count, 1, one)

    def first_side(self):
        p = self.p

        def one(d):
            z = p.outer(-d)

            def go():
                self.a_copy(d, z, p.ra).wait_recv()
                self.b_copy(d, 1, z, p.ra).start()

            self.when(self.h, z, go)

        steps_over(p.outer_count, 0, one)

    def second_side(self):
        p = self.p

        def one(d):
            z = p.outer(-d)

            def go():
                self.b_copy(d, 0, z, p.rb).wait_recv()
                self.b_copy(d, 1, z, p.rd).wait_recv()
                for i, (to, _) in enumerate(self.peers):
                    self.d_copy(d, i, z, self.h, to).start()

            self.when(self.h, z, go)

        steps_over(p.outer_count, 0, one)

    def across(self):
        p = self.p
        for i, (_, source) in enumerate(self.peers):

            def one(d, i=i, source=source):
                z = p.outer(-d)
                self.when(source, z, lambda: self.d_copy(d, i, z, source, p.n).wait_recv())

            steps_over(p.outer_count, 0, one)

    def sent(self):
        p = self.p
        self.when(
            self.h, p.z,
            lambda: steps_over(p.outer_count, 1, lambda d: self.z_copy(d, p.z, p.outer(d)).wait_send()),
        )

        def one(d):
            z = p.outer(-d)

            def go():
                self.a_copy(d, z, p.r).wait_send()
                self.b_copy(d, 0, z, p.r).wait_send()
                self.b_copy(d, 1, z, p.ra).wait_send()
                for i, (to, _) in enumerate(self.peers):
                    self.d_copy(d, i, z, self.h, to).wait_send()

            self.when(self.h, z, go)

        steps_over(p.outer_count, 0, one)


def kernel(
    wide, narrow, right, partial, window, inverse, factor, solved, trailing,
    ybuf, ibuf, xbuf, tbuf, pbuf, wbuf, fan,
    y_zs, y_zr, y_as, y_ar, y_bs, y_br, y_ds, y_dr,
    i_zs, i_zr, i_as, i_ar, i_bs, i_br, i_ds, i_dr,
    p_s, p_r, w_s, w_r, t_s, t_r, t_own,
):
    place = Place(wide, narrow)
    n = place.n
    blocks, rows, rhs = right.shape
    cols = inverse.shape[2]
    half = rhs // 2
    step_rows = wide * rows
    outer_rows = INNER * rows
    trail = trailing.shape[0]
    shifts = range(1, narrow)

    barrier = pltpu.get_barrier_semaphore()

    def greet(device):
        pl.semaphore_signal(barrier, inc=1, device_id=device, device_id_type=MESH)

    steps_over(place.outer_count, 1, lambda d: greet(place.at(place.outer(d), place.r)))
    greet(place.at(place.z, place.ra))
    greet(place.at(place.z, place.rb))
    for s in shifts:
        greet((place.w, place.side(s)))
    pl.semaphore_wait(barrier, place.outer_count - 1 + 2 + narrow - 1)

    def side_copy(src, dst, send, recv, s):
        return pltpu.make_async_remote_copy(
            src_ref=src, dst_ref=dst, send_sem=send, recv_sem=recv,
            device_id=(place.w, place.side(s)), device_id_type=MESH,
        )

    def p_copy(s, k):
        return side_copy(partial.at[0, k], pbuf.at[s - 1, k], p_s.at[s - 1, k], p_r.at[s - 1, k], s)

    def w_copy(s, slot):
        return side_copy(window, wbuf.at[slot], w_s.at[s - 1], w_r.at[s - 1], s)

    def t_copy(s, slot):
        to = place.side(s)
        return side_copy(
            factor.at[pl.ds(pl.multiple_of(to * trail, trail), trail)], tbuf.at[slot],
            t_s.at[s - 1], t_r.at[s - 1], s,
        )

    t_here = pltpu.make_async_copy(
        factor.at[pl.ds(pl.multiple_of(n * trail, trail), trail)], tbuf.at[n], t_own
    )

    for s in shifts:
        p_copy(s, 0).start()

    mate = n + 1 - 2 * place.c
    y_sems = (y_zs, y_zr, y_as, y_ar, y_bs, y_br, y_ds, y_dr)
    i_sems = (i_zs, i_zr, i_as, i_ar, i_bs, i_br, i_ds, i_dr)
    everyone = [(place.side(s), place.side(-s)) for s in shifts]
    ys = [Gather(place, ybuf, y_sems, k, place.c, [(mate, 1 - place.c)]) for k in range(blocks)]
    needed = lambda h, z: z * outer_rows < (h + 1) * cols
    inv = [Gather(place, ibuf, i_sems, k, n, everyone, needed) for k in range(blocks)]

    ibuf[0, n, place.z, place.r] = inverse[0]
    inv[0].own()

    def residue(k):
        fanned = partial[0, k]
        for s in shifts:
            fanned = fanned + pbuf[s - 1, k]
        if k > 0:
            fanned = fanned + fan[...]
        value = (right[k].astype(F32) - fanned).astype(BF16)
        for c in range(2):

            @pl.when(place.c == c)
            def _():
                ybuf[k, c, place.z, place.r] = value[:, c * half:(c + 1) * half]

    for s in shifts:
        p_copy(s, 0).wait_recv()
    residue(0)
    ys[0].own()

    for s in shifts:
        for k in range(1, blocks):
            p_copy(s, k).start()
        w_copy(s, n).start()
        t_copy(s, n).start()
    t_here.start()
    for k in range(1, blocks):
        ibuf[k, n, place.z, place.r] = inverse[k]
    wbuf[n] = window[...]

    width = min(256, cols)

    def solve(k):
        for h in range(narrow):
            deep = min(place.outer_count, -(-(h + 1) * cols // outer_rows))

            def tile(t, h=h, deep=deep):
                at = pl.multiple_of(t * width, width)
                lhs = ibuf[k, h, :deep, :, :, pl.ds(at, width)].reshape(deep * outer_rows, width)
                for c in range(2):
                    rhs_part = ybuf[k, c, :deep].reshape(deep * outer_rows, half)
                    out = lax.dot_general(lhs, rhs_part, (((0,), (0,)), ((), ())), preferred_element_type=F32)
                    xbuf[k, pl.ds(pl.multiple_of(h * cols + at, width), width), c * half:(c + 1) * half] = out.astype(BF16)

            lax.fori_loop(0, cols // width, lambda t, carry: (tile(t), carry)[1], 0)

    def fan_in(k, j):
        total = None
        for h in range(narrow):
            term = jnp.dot(
                wbuf[h, k * (k - 1) // 2 + j], xbuf[j, h * cols:(h + 1) * cols, :], preferred_element_type=F32
            )
            total = term if total is None else total + term
        if j == 0:
            fan[...] = total
        else:
            fan[...] += total

    high = min(256, trail)

    def trail_in(k):
        def tile(t):
            at = pl.ds(pl.multiple_of(t * high, high), high)
            total = None
            for h in range(narrow):
                term = jnp.dot(tbuf[h, at, k, :], xbuf[k, h * cols:(h + 1) * cols, :], preferred_element_type=F32)
                total = term if total is None else total + term
            if k == 0:
                trailing[at, :] = total
            else:
                trailing[at, :] += total

        lax.fori_loop(0, trail // high, lambda t, carry: (tile(t), carry)[1], 0)

    if blocks > 1:
        inv[1].own()
    inv[0].line()
    ys[0].line()
    inv[0].first_side()
    for k in range(blocks):
        y, last = ys[k], k == blocks - 1
        if k > 0:
            y.line()
        y.first_side()
        if k == 0:
            inv[0].second_side()
            if not last:
                inv[1].line()
        if not last:
            inv[k + 1].first_side()
        if k + 2 < blocks:
            inv[k].sent()
            inv[k + 2].own()
        if k == 1:
            for s in shifts:
                t_copy(s, place.side(-s)).wait_recv()
            t_here.wait()
        if k > 0:
            trail_in(k - 1)
            if not last:
                for j in range(k):
                    fan_in(k + 1, j)
        y.second_side()
        inv[k].across()
        y.across()
        solve(k)
        y.sent()
        if not last:
            if k == 0:
                for s in shifts:
                    w_copy(s, place.side(-s)).wait_recv()
                    for later in range(1, blocks):
                        p_copy(s, later).wait_recv()
            fan_in(k + 1, k)
            residue(k + 1)
            ys[k + 1].own()
            inv[k + 1].second_side()
        if k + 2 < blocks:
            inv[k + 2].line()
    for k in range(max(0, blocks - 2), blocks):
        inv[k].sent()
    trail_in(blocks - 1)
    for h in range(narrow):

        @pl.when(n == h)
        def _():
            for k in range(blocks):
                solved[k] = xbuf[k, h * cols:(h + 1) * cols, :]

    for s in shifts:
        for k in range(blocks):
            p_copy(s, k).wait_send()
        w_copy(s, n).wait_send()
        t_copy(s, n).wait_send()


def per_device(wide, narrow, right_side, partial_in, window_factor, inverse_t, trailing_factor):
    blocks, rows, rhs = right_side.shape
    cols = inverse_t.shape[2]
    trail = trailing_factor.shape[0] // narrow
    outer = wide // INNER
    window = jnp.stack([window_factor[k, :, j, :] for k in range(blocks) for j in range(k)])
    factor = trailing_factor
    dma = pltpu.SemaphoreType.DMA

    def gather_sems(peers):
        return [
            dma((2, outer)), dma((blocks, outer)),
            dma((2, outer)), dma((blocks, outer)),
            dma((2, 2, outer)), dma((blocks, 2, outer)),
            dma((2, peers, outer)), dma((blocks, peers, outer)),
        ]

    vmem = pl.BlockSpec(memory_space=pltpu.VMEM)
    step_rows = wide * rows
    return pl.pallas_call(
        functools.partial(kernel, wide, narrow),
        out_shape=(
            jax.ShapeDtypeStruct((blocks, cols, rhs), BF16),
            jax.ShapeDtypeStruct((trail, rhs), F32),
        ),
        in_specs=[vmem, vmem, vmem, vmem, pl.BlockSpec(memory_space=pl.ANY)],
        out_specs=(vmem, vmem),
        scratch_shapes=[
            pltpu.VMEM((blocks, 2, outer, INNER, rows, rhs // 2), BF16),
            pltpu.VMEM((blocks, narrow, outer, INNER, rows, cols), BF16),
            pltpu.VMEM((blocks, step_rows, rhs), BF16),
            pltpu.VMEM((narrow, trail, blocks, cols), BF16),
            pltpu.VMEM((narrow - 1, blocks, rows, rhs), F32),
            pltpu.VMEM((narrow, blocks * (blocks - 1) // 2, rows, cols), BF16),
            pltpu.VMEM((rows, rhs), F32),
            *gather_sems(1),
            *gather_sems(narrow - 1),
            dma((narrow - 1, blocks)), dma((narrow - 1, blocks)),
            dma((narrow - 1,)), dma((narrow - 1,)),
            dma((narrow - 1,)), dma((narrow - 1,)),
            dma,
        ],
        compiler_params=pltpu.CompilerParams(
            collective_id=0, has_side_effects=True, vmem_limit_bytes=56 * 1024 * 1024
        ),
    )(right_side, partial_in, window, inverse_t, factor)


def solution(mesh):
    placed = (
        P(None, "wide", None),
        P("narrow", None, "wide", None),
        P(None, "wide", None, "narrow"),
        P(None, "wide", "narrow"),
        P("wide", None, "narrow"),
    )
    return jax.shard_map(
        functools.partial(per_device, mesh.shape["wide"], mesh.shape["narrow"]),
        mesh=mesh,
        in_specs=placed,
        out_specs=(P(None, "narrow", None), P(("wide", "narrow"), None)),
        check_vma=False,
    )
```
